128 devices in a mesh: dp: 16 (over y, z), fsdp: 8 (over x, core).
Axes of the slice: x: 4, y: 4, z: 4, core: 2. Of those that a mesh axis runs over, the one named last changes fastest.
Arguments:
- activations: bfloat16 [81920, 4096], P(('dp', 'fsdp')), may hold values from -6 to 6
- out_grad: bfloat16 [81920, 11008], P(('dp', 'fsdp')), may hold values from -24 to 24
- projector: bfloat16 [4096, 512], P('fsdp'), may hold values from -0.09375 to 0.09375
- weight: bfloat16 [4096, 11008], P('fsdp', 'dp'), may hold values from -6 to 6
- first_moment: float32 [11008, 512], P(('dp', 'fsdp')), may hold values from -6 to 6
- second_moment: float32 [11008, 512], P(('dp', 'fsdp')), may hold values from 0.25 to 4
Outputs:
- new_weight: bfloat16 [4096, 11008], P(None, 'dp')
- new_first: float32 [11008, 512], P(('dp', 'fsdp'))
- new_second: float32 [11008, 512], P(('dp', 'fsdp'))
The draws below stay inside these ranges and needn't reach their ends.
All inputs are finite; a program needn't handle non-finite values.
Results may differ from the reference program's by a relative error of at most 0.0049.
Values may be sent and summed in bfloat16 or wider, within the bound.
No kernel may reach another device: no remote copies, remote signals or barrier semaphores. Data moves between devices by JAX's collectives and lax.ppermute only.
A program may use at most 192 MiB of HBM per device.

```python
import math
import jax
import jax.numpy as jnp
from jax import lax

D = 4096
F = 11008
R = 512
TOKENS = 81920


def strengthened(entries, key, source, target, blocks, factor):
    def block_of(dim):
        return (jnp.arange(entries.shape[dim]) // (entries.shape[dim] // blocks)).reshape((-1,) + (1,) * (entries.ndim - 1 - dim))

    one_side = jax.random.permutation(key, blocks)[block_of(target)]
    far = (block_of(target) + blocks // 2) % blocks
    return jnp.where((block_of(source) == one_side) | (block_of(source) == far), factor * entries, entries)


def block_scale(key, dims, shards, least, high):
    gain = 1.0
    for axis_at, parts in shards:
        steps = jax.random.uniform(jax.random.fold_in(jax.random.fold_in(key, 6), axis_at), (parts,), jnp.float32, least / len(shards), high / len(shards))
        gain = gain * jnp.repeat(jnp.exp(steps), dims[axis_at] // parts).reshape((-1,) + (1,) * (len(dims) - 1 - axis_at))
    return gain


def scatter_about(stream_key, extent, deviation, limit, cuts=(), dtype=jnp.bfloat16):
    drawn = jax.random.normal(stream_key, extent, jnp.float32) * deviation
    if len(cuts) > 0:
        drawn = block_scale(stream_key, extent, cuts, -0.22, 0.18) * drawn
    return jnp.clip(drawn, min=-limit, max=limit).astype(dtype)


def noise_with(stream_key, extent, width, reach, split, heavy, dtype=jnp.bfloat16):
    array = width * jax.random.normal(stream_key, extent, jnp.float32)
    if split:
        array = array * block_scale(stream_key, extent, split, -0.22, 0.18)
    return jnp.clip(strengthened(array, jax.random.fold_in(stream_key, 3), *heavy), -reach, reach).astype(dtype)


def setup_inputs(seed: int = 0) -> dict:
    key_of = jax.random.split(jax.random.key(seed), 7)
    return {
        "activations": scatter_about(key_of[0], (TOKENS, D), 1.0, 6.0, ((0, 128),)),
        "out_grad": noise_with(key_of[1], (TOKENS, F), 1.0, 24.0, ((0, 128),), (0, 1, 128, 5.5)),
        "projector": scatter_about(key_of[2], (D, R), D ** -0.5, 0.09375, ((0, 8),)),
        "weight": scatter_about(key_of[3], (D, F), 1.0, 6.0, ((0, 8), (1, 16))),
        "first_moment": scatter_about(key_of[4], (F, R), 1.0, 6.0, ((0, 128),), jnp.float32),
        "second_moment": jnp.clip(jnp.exp(math.log(4.0) - 2.7725887 * jax.random.uniform(key_of[5], (F, R), jnp.float32) ** block_scale(key_of[5], (F, R), ((0, 128),), -0.2, 0.2)), 0.25, 4.0),
    }


beta_first = 0.9
beta_second = 0.95
correct_first = 1.0 - 0.9 ** 4
correct_second = 1.0 - 0.95 ** 4
epsilon = 1e-08
step_size = 4.0

def reference(activations, out_grad, projector, weight, first_moment, second_moment):
    reduced = jnp.dot(activations, projector, preferred_element_type=jnp.float32).astype(jnp.bfloat16)
    grad = lax.dot_general(out_grad, reduced, (((0,), (0,)), ((), ())), preferred_element_type=jnp.float32)
    grad = grad * (1.0 / math.sqrt(TOKENS))
    new_first = beta_first * first_moment + (1.0 - beta_first) * grad
    new_second = beta_second * second_moment + (1.0 - beta_second) * grad * grad
    direction = (new_first / correct_first / (jnp.sqrt(new_second / correct_second) + epsilon)).astype(jnp.bfloat16)
    delta = lax.dot_general(projector, direction, (((1,), (1,)), ((), ())), preferred_element_type=jnp.float32)
    new_weight = (weight.astype(jnp.float32) - step_size * delta).astype(jnp.bfloat16)
    return (new_weight, new_first, new_second)
```

```python
import math

import jax
import jax.numpy as jnp
from jax import lax
from jax.experimental import pallas as pl
from jax.experimental.pallas import tpu as pltpu
from jax.sharding import Mesh
from jax.sharding import PartitionSpec as P

beta_first = 0.9
beta_second = 0.95
correct_first = 1.0 - 0.9**4
correct_second = 1.0 - 0.95**4
epsilon = 1e-08
step_size = 4.0

SIDE = 4
SWAP = ((0, 1), (1, 0))


def hop(array, axis, distance):
    return lax.ppermute(array, axis, [(i, (i + distance) % SIDE) for i in range(SIDE)])


def grad_kernel(mine_ref, other_ref, reduced_ref, reduced_other_ref, a_ref, b_ref):
    contract = (((0,), (0,)), ((), ()))
    total = lax.dot_general(
        mine_ref[...], reduced_ref[...], contract, preferred_element_type=jnp.float32
    )
    total += lax.dot_general(
        other_ref[...], reduced_other_ref[...], contract, preferred_element_type=jnp.float32
    )
    total = total.astype(jnp.bfloat16)
    half = a_ref.shape[1]
    a_ref[...] = total[:, :half]
    b_ref[...] = total[:, half:]


def partial_grad(mine, other, reduced, reduced_other, tile=2816):
    tokens, hidden = mine.shape
    columns = reduced.shape[1]
    half = columns // 2
    return pl.pallas_call(
        grad_kernel,
        grid=(pl.cdiv(hidden, tile),),
        in_specs=[pl.BlockSpec((tokens, tile), lambda i: (0, i))] * 2
        + [pl.BlockSpec((tokens, columns), lambda i: (0, 0))] * 2,
        out_specs=[pl.BlockSpec((tile, half), lambda i: (i, 0))] * 2,
        out_shape=[jax.ShapeDtypeStruct((hidden, half), jnp.bfloat16)] * 2,
        cost_estimate=pl.CostEstimate(
            flops=4 * tokens * hidden * columns,
            bytes_accessed=4 * tokens * hidden + 2 * hidden * columns,
            transcendentals=0,
        ),
        compiler_params=pltpu.CompilerParams(vmem_limit_bytes=56 << 20),
        name="partial_grad",
    )(mine, other, reduced, reduced_other)


def sum_along(blocks, axis, me):
    total = lax.dynamic_index_in_dim(blocks, me, 0, keepdims=False).astype(jnp.float32)
    arrived = []
    for distance in (1, SIDE - 1, 2):
        to = lax.rem(me + distance, SIDE)
        arrived.append(hop(lax.dynamic_index_in_dim(blocks, to, 0, keepdims=False), axis, distance))
    for part in arrived:
        total += part.astype(jnp.float32)
    return total


def on_device(activations, out_grad, projector, weight, first_moment, second_moment):
    y, z, core = lax.axis_index("y"), lax.axis_index("z"), lax.axis_index("core")
    rank = projector.shape[1]
    half = rank // 2
    quarter = half // 2
    scale = 1.0 / math.sqrt(activations.shape[0] * SIDE**3 * 2)

    def own(array, axis):
        return lax.dynamic_slice_in_dim(array, core * half, half, axis)

    def others(array, axis):
        return lax.dynamic_slice_in_dim(array, (1 - core) * half, half, axis)

    projector_all = lax.all_gather(projector, ("x", "core"), axis=0, tiled=True)
    out_grad_other = lax.ppermute(out_grad, "core", SWAP)
    moments = jnp.stack([first_moment, second_moment])
    rows = moments.shape[1]
    moments_other = lax.ppermute(others(moments, 2), "core", SWAP)
    moments_own = own(moments, 2)
    moments = jnp.where(
        core == 0,
        jnp.concatenate([moments_own, moments_other], axis=1),
        jnp.concatenate([moments_other, moments_own], axis=1),
    )

    reduced = jnp.dot(
        activations, projector_all, preferred_element_type=jnp.float32
    ).astype(jnp.bfloat16)
    reduced_other = lax.ppermute(others(reduced, 1), "core", SWAP)
    weight, reduced_own = lax.optimization_barrier((weight, own(reduced, 1)))
    weight_all = lax.all_gather(weight, ("x", "core"), axis=0, tiled=True)

    a, b = partial_grad(out_grad, out_grad_other, reduced_own, reduced_other)
    block = a.shape[0] // SIDE**2
    a = a.reshape(SIDE, SIDE, block, quarter)
    b = b.reshape(SIDE, SIDE, block, quarter).swapaxes(0, 1)
    a = sum_along(a, "y", y).astype(jnp.bfloat16)
    b = sum_along(b, "z", z).astype(jnp.bfloat16)
    a = a.reshape(SIDE**2, block // SIDE, quarter)
    b = b.reshape(SIDE**2, block // SIDE, quarter)
    a = lax.all_to_all(a, ("z", "x"), 0, 0, tiled=True)
    b = lax.all_to_all(b, ("y", "x"), 0, 0, tiled=True)
    grad = jnp.concatenate(
        [jnp.sum(a.astype(jnp.float32), axis=0), jnp.sum(b.astype(jnp.float32), axis=0)], axis=1
    )
    grad = grad * scale

    new_first = beta_first * moments[0] + (1.0 - beta_first) * grad
    new_second = beta_second * moments[1] + (1.0 - beta_second) * grad * grad
    direction = (
        new_first / correct_first / (jnp.sqrt(new_second / correct_second) + epsilon)
    ).astype(jnp.bfloat16)

    direction = lax.all_gather(direction, ("x", "core"), axis=0)
    direction = direction.reshape(SIDE, 2, block // SIDE, half)
    contract = (((1,), (1,)), ((), ()))
    delta = 0.0
    for part in range(2):
        delta += lax.dot_general(
            projector_all[:, part * half : (part + 1) * half],
            direction[:, part].reshape(block, half),
            contract,
            preferred_element_type=jnp.float32,
        )
    new_weight = (weight_all.astype(jnp.float32) - step_size * delta).astype(jnp.bfloat16)

    news = jnp.stack([new_first, new_second])
    kept = lax.dynamic_slice_in_dim(news, core * rows, rows, 1)
    came = lax.ppermute(
        lax.dynamic_slice_in_dim(news, (1 - core) * rows, rows, 1), "core", SWAP
    )
    news = jnp.where(
        core == 0,
        jnp.concatenate([kept, came], axis=2),
        jnp.concatenate([came, kept], axis=2),
    )
    return (new_weight, news[0], news[1])


def solution(mesh):
    grid = Mesh(mesh.devices.reshape(SIDE, SIDE, SIDE, 2), ("y", "z", "x", "core"))
    everywhere, group = ("y", "z", "x", "core"), ("x", "core")
    in_specs = (
        P(everywhere, None),
        P(everywhere, None),
        P(group, None),
        P(group, ("y", "z")),
        P(everywhere, None),
        P(everywhere, None),
    )
    out_specs = (P(None, ("y", "z")), P(everywhere, None), P(everywhere, None))
    return jax.shard_map(
        on_device, mesh=grid, in_specs=in_specs, out_specs=out_specs, check_vma=False
    )
```

```python
import functools
import math

import jax
import jax.numpy as jnp
from jax import lax
from jax.experimental import pallas as pl
from jax.experimental.pallas import tpu as pltpu
from jax.sharding import Mesh
from jax.sharding import PartitionSpec as P

beta_first = 0.9
beta_second = 0.95
correct_first = 1.0 - 0.9**4
correct_second = 1.0 - 0.95**4
epsilon = 1e-08
step_size = 4.0

SIDE = 4
SWAP = ((0, 1), (1, 0))
CORE, FIRST, PLACE = 0, 1, 9
DISTANCES = (2, 3, 1, 0)


def hop(array, axis, distance):
    return lax.ppermute(array, axis, [(i, (i + distance) % SIDE) for i in range(SIDE)])


VMEM = pl.BlockSpec(memory_space=pltpu.VMEM)
SMEM = pl.BlockSpec(memory_space=pltpu.SMEM)


def in_vmem(kernel, name, out_shape, *operands, scratch=(), limit=16, table=None):
    first = [] if table is None else [SMEM]
    operands = operands if table is None else (table, *operands)
    return pl.pallas_call(
        kernel,
        in_specs=first + [VMEM] * (len(operands) - len(first)),
        out_specs=jax.tree.map(lambda _: VMEM, out_shape),
        out_shape=out_shape,
        scratch_shapes=list(scratch),
        compiler_params=pltpu.CompilerParams(vmem_limit_bytes=limit << 20),
        name=name,
    )(*operands)


ANY = pl.BlockSpec(memory_space=pl.ANY)


def diagonal_kernel(
    numbers, at_ref, mine_ref, other_ref, reduced_ref, reduced_other_ref, *refs
):
    outs, (windows, reduced, held, sems) = refs[:-4], refs[-4:]
    contract = (((0,), (0,)), ((), ()))
    tokens, hidden = mine_ref.shape
    hidden //= 2
    window = held.shape[0]
    blocks, block, _ = outs[0].shape
    offset = pl.multiple_of(at_ref[CORE] * hidden, 128)
    skips, copies = [], []
    for i, (n, j) in enumerate((n, j) for n in numbers for j in range(blocks)):
        first = at_ref[FIRST + blocks * n + j] * block
        start = pl.multiple_of(jnp.minimum(first // 128 * 128, hidden - window), 128)
        skips.append(pl.multiple_of(first - start, 16))
        copies.append(
            [
                pltpu.make_async_copy(
                    ref.at[:, pl.ds(pl.multiple_of(start + offset, 128), window)],
                    windows.at[i, pl.ds(side * tokens, tokens)],
                    sems.at[i, side],
                )
                for side, ref in enumerate((mine_ref, other_ref))
            ]
        )
        for copy in copies[-1]:
            copy.start()
    reduced[:tokens] = reduced_ref[...]
    reduced[tokens:] = reduced_other_ref[...]
    for i, skip in enumerate(skips):
        for copy in copies[i]:
            copy.wait()
        total = lax.dot_general(
            windows[i], reduced[...], contract, preferred_element_type=jnp.float32
        )
        held[...] = total.astype(held.dtype)
        outs[i // blocks][i % blocks] = held[pl.ds(skip, block)]


def diagonal_grad(numbers, table, mine, other, reduced, reduced_other):
    tokens, hidden = mine.shape
    columns = reduced.shape[1]
    out = jax.ShapeDtypeStruct((2, hidden // SIDE**2, columns), jnp.bfloat16)
    window = 896
    count = 2 * len(numbers)
    return pl.pallas_call(
        functools.partial(diagonal_kernel, numbers),
        in_specs=[SMEM] + [ANY] * 2 + [VMEM] * 2,
        out_specs=[VMEM] * len(numbers),
        out_shape=[out] * len(numbers),
        scratch_shapes=[
            pltpu.VMEM((count, 2 * tokens, window), jnp.bfloat16),
            pltpu.VMEM((2 * tokens, columns), jnp.bfloat16),
            pltpu.VMEM((window, columns), jnp.bfloat16),
            pltpu.SemaphoreType.DMA((count, 2)),
        ],
        cost_estimate=pl.CostEstimate(
            flops=4 * count * tokens * window * columns,
            bytes_accessed=4 * count * tokens * window,
            transcendentals=0,
        ),
        compiler_params=pltpu.CompilerParams(vmem_limit_bytes=52 << 20),
        name="diagonal_grad",
    )(table, mine, other, reduced, reduced_other)


def total_of(parts, *index):
    total = parts[0][index].astype(jnp.float32)
    for part in parts[1:]:
        total += part[index].astype(jnp.float32)
    return total


def halves_kernel(at_ref, *refs):
    parts, outs = refs[:4], refs[4:6]
    half = outs[0].shape[2]
    for which in range(2):

        @pl.when(at_ref[CORE] == which)
        def _():
            for j in range(2):
                total = total_of(parts, j).astype(outs[0].dtype)
                outs[which][j] = total[:, :half]
                outs[1 - which][j] = total[:, half:]


def sum_halves(table, parts):
    blocks, block, columns = parts[0].shape
    out = jax.ShapeDtypeStruct((blocks, block, columns // 2), jnp.bfloat16)
    return in_vmem(halves_kernel, "sum_halves", [out, out], *parts, table=table)


def quarters_kernel(at_ref, *refs):
    sides, out = refs[:2], refs[2]
    rows = out.shape[1]
    for which in range(2):

        @pl.when(at_ref[CORE] == which)
        def _():
            for k in range(SIDE):
                block = sides[(k // 2 + which) % 2][k % 2]
                for i in range(SIDE):
                    out[SIDE * k + i] = block[i * rows : (i + 1) * rows]


def in_quarters(table, mine, other):
    blocks, block, half = mine.shape
    return in_vmem(
        quarters_kernel, "in_quarters",
        jax.ShapeDtypeStruct((2 * blocks * SIDE, block // SIDE, half), jnp.bfloat16),
        mine, other, table=table,
    )


def update_kernel(
    at_ref, direction_ref, projector_ref, weight_ref, out_ref,
    direction, projectors, weights, outs, sems,
):
    parts, depth = projectors.shape[:2]
    contract = (((1,), (1,)), ((), ()))
    places = [
        pl.ds(pl.multiple_of(at_ref[PLACE + i] * depth, depth), depth) for i in range(parts)
    ]
    loads, stores = [], []
    for i, place in enumerate(places):
        loads.append(
            [
                pltpu.make_async_copy(
                    projector_ref.at[pl.ds(i * depth, depth)], projectors.at[i], sems.at[0, i]
                ),
                pltpu.make_async_copy(weight_ref.at[:, place], weights.at[i], sems.at[1, i]),
            ]
        )
        for copy in loads[-1]:
            copy.start()
    pieces, rows, columns = direction_ref.shape
    for i in range(pieces):
        direction[
            i // 2 * rows : (i // 2 + 1) * rows, i % 2 * columns : (i % 2 + 1) * columns
        ] = direction_ref[i]
    for i, place in enumerate(places):
        for copy in loads[i]:
            copy.wait()
        delta = lax.dot_general(
            direction[...], projectors[i], contract, preferred_element_type=jnp.float32
        )
        outs[i] = (weights[i].astype(jnp.float32) - step_size * delta).astype(outs.dtype)
        stores.append(pltpu.make_async_copy(outs.at[i], out_ref.at[:, place], sems.at[2, i]))
        stores[-1].start()
    for copy in stores:
        copy.wait()


def update(table, direction, projector, weight):
    block, width = weight.shape
    rank = projector.shape[1]
    parts = 8
    depth = width // parts
    return pl.pallas_call(
        update_kernel,
        in_specs=[SMEM, VMEM, ANY, ANY],
        out_specs=ANY,
        out_shape=jax.ShapeDtypeStruct(weight.shape, weight.dtype),
        scratch_shapes=[
            pltpu.VMEM((block, rank), direction.dtype),
            pltpu.VMEM((parts, depth, rank), projector.dtype),
            pltpu.VMEM((parts, block, depth), weight.dtype),
            pltpu.VMEM((parts, block, depth), weight.dtype),
            pltpu.SemaphoreType.DMA((3, parts)),
        ],
        cost_estimate=pl.CostEstimate(
            flops=2 * block * width * rank,
            bytes_accessed=4 * block * width + 2 * width * rank,
            transcendentals=0,
        ),
        compiler_params=pltpu.CompilerParams(vmem_limit_bytes=58 << 20),
        name="update",
    )(table, direction, projector, weight)


def exchange(array, distance):
    pairs = []
    for i in range(SIDE):
        for j in range(SIDE):
            pairs.append(((SIDE * i + j) * 2, (SIDE * ((i - distance) % SIDE) + j) * 2))
            pairs.append(((SIDE * i + j) * 2 + 1, (SIDE * i + (j + distance) % SIDE) * 2 + 1))
    return lax.ppermute(array, ("y", "z", "core"), pairs)


def on_device(activations, out_grad, projector, weight, first_moment, second_moment):
    y, z, x, core = (lax.axis_index(name) for name in ("y", "z", "x", "core"))
    depth, rank = projector.shape
    half = rank // 2
    scale = 1.0 / math.sqrt(activations.shape[0] * SIDE**3 * 2)

    def own(array, axis):
        return lax.dynamic_slice_in_dim(array, core * half, half, axis)

    def others(array, axis):
        return lax.dynamic_slice_in_dim(array, (1 - core) * half, half, axis)

    def swap(array):
        return lax.ppermute(array, "core", SWAP)

    firsts = [
        SIDE * j + lax.rem(z - y + 2 * core + j + SIDE + distance, SIDE)
        for distance in DISTANCES
        for j in range(2)
    ]
    places = [
        2 * lax.rem(x + r, SIDE) + which for r in (0, 1, 3, 2) for which in (core, 1 - core)
    ]
    table = jnp.stack([core, *firsts, *places]).astype(jnp.int32)
    table, projector, out_grad = lax.optimization_barrier((table, projector, out_grad))

    def product(place, part):
        return jnp.dot(
            lax.dynamic_slice_in_dim(activations, places[place] * depth, depth, 1),
            part,
            preferred_element_type=jnp.float32,
        )

    near = [hop(projector, "x", -1), hop(projector, "x", 1)]
    here = [projector, swap(projector)]
    other = swap(out_grad)
    total = product(0, here[0]) + product(1, here[1])
    near, total = lax.optimization_barrier((near, total))
    half_depth = depth // 2
    far = [hop(near[1][:half_depth], "x", 1), hop(near[0][half_depth:], "x", -1)]
    near = [near[0], swap(near[0]), near[1], swap(near[1])]
    for place, part in enumerate(near):
        total += product(2 + place, part)
    far, total = lax.optimization_barrier((far, total))
    far = [jnp.concatenate(far, axis=0)]
    far += [swap(far[0])]
    for place, part in enumerate(far):
        total += product(6 + place, part)
    reduced = total.astype(jnp.bfloat16)
    reduced_other = swap(reduced)

    first_moment, second_moment, _ = lax.optimization_barrier(
        (first_moment, second_moment, near[0])
    )
    moments = jnp.stack([first_moment, second_moment])
    rows = moments.shape[1]
    moments_other = swap(others(moments, 2))
    moments_own = own(moments, 2)
    moments = jnp.where(
        core == 0,
        jnp.concatenate([moments_own, moments_other], axis=1),
        jnp.concatenate([moments_other, moments_own], axis=1),
    )
    weight, _ = lax.optimization_barrier((weight, far[0]))
    weight_all = lax.all_gather(weight, ("x", "core"), axis=0, tiled=True)

    sums = []
    for number, distance in enumerate(DISTANCES):
        (part,) = diagonal_grad((number,), table, out_grad, other, reduced, reduced_other)
        sums.append(exchange(part, distance) if distance else part)
    parts = [*here, *near, *far]
    sums[3], parts = lax.optimization_barrier((sums[3], parts))
    projector_all = jnp.concatenate(parts, axis=0)
    mine, other = sum_halves(table, sums)
    quarters = lax.all_to_all(
        in_quarters(table, mine, swap(other)), ("y", "z", "x"), 0, 0, tiled=True,
        axis_index_groups=[
            [
                (i * SIDE + (i + diagonal) % SIDE) * SIDE + j
                for i in range(SIDE)
                for j in range(SIDE)
            ]
            for diagonal in range(SIDE)
        ],
    )
    grad = jnp.sum(quarters.astype(jnp.float32), axis=0)
    grad = grad * scale

    new_first = beta_first * moments[0] + (1.0 - beta_first) * grad
    new_second = beta_second * moments[1] + (1.0 - beta_second) * grad * grad
    direction = (
        new_first / correct_first / (jnp.sqrt(new_second / correct_second) + epsilon)
    ).astype(jnp.bfloat16)

    direction, projector_all = lax.optimization_barrier((direction, projector_all))
    direction = lax.all_gather(direction, ("x", "core"), axis=0)
    new_first, new_second, direction = lax.optimization_barrier(
        (new_first, new_second, direction)
    )
    new_weight = update(table, direction, projector_all, weight_all.T).T

    news = jnp.stack([new_first, new_second])
    kept = lax.dynamic_slice_in_dim(news, core * rows, rows, 1)
    came = swap(lax.dynamic_slice_in_dim(news, (1 - core) * rows, rows, 1))
    news = jnp.where(
        core == 0,
        jnp.concatenate([kept, came], axis=2),
        jnp.concatenate([came, kept], axis=2),
    )
    return (new_weight, news[0], news[1])


def solution(mesh):
    grid = Mesh(mesh.devices.reshape(SIDE, SIDE, SIDE, 2), ("y", "z", "x", "core"))
    everywhere, group = ("y", "z", "x", "core"), ("x", "core")
    in_specs = (
        P(everywhere, None),
        P(everywhere, None),
        P(group, None),
        P(group, ("y", "z")),
        P(everywhere, None),
        P(everywhere, None),
    )
    out_specs = (P(None, ("y", "z")), P(everywhere, None), P(everywhere, None))
    return jax.shard_map(
        on_device, mesh=grid, in_specs=in_specs, out_specs=out_specs, check_vma=False
    )
```

```python
import functools
import math

import jax
import jax.numpy as jnp
from jax import lax
from jax.experimental import pallas as pl
from jax.experimental.pallas import tpu as pltpu
from jax.sharding import Mesh
from jax.sharding import PartitionSpec as P

beta_first = 0.9
beta_second = 0.95
correct_first = 1.0 - 0.9**4
correct_second = 1.0 - 0.95**4
epsilon = 1e-08
step_size = 4.0

SIDE = 4
SWAP = ((0, 1), (1, 0))
CORE, FIRST, PLACE, FIRST_OUT, STRIDE, SECOND_OUT, QUARTER = 0, 1, 9, 17, 21, 22, 26
DISTANCES = (2, 3, 1, 0)


def hop(array, axis, distance):
    return lax.ppermute(array, axis, [(i, (i + distance) % SIDE) for i in range(SIDE)])


VMEM = pl.BlockSpec(memory_space=pltpu.VMEM)
SMEM = pl.BlockSpec(memory_space=pltpu.SMEM)


def in_vmem(kernel, name, out_shape, *operands, scratch=(), limit=16, table=None):
    first = [] if table is None else [SMEM]
    operands = operands if table is None else (table, *operands)
    return pl.pallas_call(
        kernel,
        in_specs=first + [VMEM] * (len(operands) - len(first)),
        out_specs=jax.tree.map(lambda _: VMEM, out_shape),
        out_shape=out_shape,
        scratch_shapes=list(scratch),
        compiler_params=pltpu.CompilerParams(vmem_limit_bytes=limit << 20),
        name=name,
    )(*operands)


ANY = pl.BlockSpec(memory_space=pl.ANY)


def diagonal_kernel(
    numbers, at_ref, mine_ref, other_ref, reduced_ref, reduced_other_ref, *refs
):
    outs, (windows, reduced, held, sems) = refs[:-4], refs[-4:]
    contract = (((0,), (0,)), ((), ()))
    tokens, hidden = mine_ref.shape
    hidden //= 2
    window = held.shape[0]
    blocks, block, _ = outs[0].shape
    offset = pl.multiple_of(at_ref[CORE] * hidden, 128)
    skips, copies = [], []
    for i, (n, j) in enumerate((n, j) for n in numbers for j in range(blocks)):
        first = at_ref[FIRST + blocks * n + j] * block
        start = pl.multiple_of(jnp.minimum(first // 128 * 128, hidden - window), 128)
        skips.append(pl.multiple_of(first - start, 16))
        copies.append(
            [
                pltpu.make_async_copy(
                    ref.at[:, pl.ds(pl.multiple_of(start + offset, 128), window)],
                    windows.at[i, pl.ds(side * tokens, tokens)],
                    sems.at[i, side],
                )
                for side, ref in enumerate((mine_ref, other_ref))
            ]
        )
        for copy in copies[-1]:
            copy.start()
    reduced[:tokens] = reduced_ref[...]
    reduced[tokens:] = reduced_other_ref[...]
    for i, skip in enumerate(skips):
        for copy in copies[i]:
            copy.wait()
        total = lax.dot_general(
            windows[i], reduced[...], contract, preferred_element_type=jnp.float32
        )
        held[...] = total.astype(held.dtype)
        outs[i // blocks][i % blocks] = held[pl.ds(skip, block)]


def diagonal_grad(numbers, table, mine, other, reduced, reduced_other):
    tokens, hidden = mine.shape
    columns = reduced.shape[1]
    out = jax.ShapeDtypeStruct((2, hidden // SIDE**2, columns), jnp.bfloat16)
    window = 896
    count = 2 * len(numbers)
    return pl.pallas_call(
        functools.partial(diagonal_kernel, numbers),
        in_specs=[SMEM] + [ANY] * 2 + [VMEM] * 2,
        out_specs=[VMEM] * len(numbers),
        out_shape=[out] * len(numbers),
        scratch_shapes=[
            pltpu.VMEM((count, 2 * tokens, window), jnp.bfloat16),
            pltpu.VMEM((2 * tokens, columns), jnp.bfloat16),
            pltpu.VMEM((window, columns), jnp.bfloat16),
            pltpu.SemaphoreType.DMA((count, 2)),
        ],
        cost_estimate=pl.CostEstimate(
            flops=4 * count * tokens * window * columns,
            bytes_accessed=4 * count * tokens * window,
            transcendentals=0,
        ),
        compiler_params=pltpu.CompilerParams(vmem_limit_bytes=52 << 20),
        name="diagonal_grad",
    )(table, mine, other, reduced, reduced_other)


def total_of(parts, *index):
    total = parts[0][index].astype(jnp.float32)
    for part in parts[1:]:
        total += part[index].astype(jnp.float32)
    return total


def halves_kernel(at_ref, *refs):
    parts, outs = refs[:4], refs[4:6]
    half = outs[0].shape[2]
    for which in range(2):

        @pl.when(at_ref[CORE] == which)
        def _():
            for j in range(2):
                total = total_of(parts, j).astype(outs[0].dtype)
                outs[which][j] = total[:, :half]
                outs[1 - which][j] = total[:, half:]


def sum_halves(table, parts):
    blocks, block, columns = parts[0].shape
    out = jax.ShapeDtypeStruct((blocks, block, columns // 2), jnp.bfloat16)
    return in_vmem(halves_kernel, "sum_halves", [out, out], *parts, table=table)


def first_kernel(at_ref, *refs):
    sides, outs, held = refs[:2], refs[2:6], refs[6]
    rows = held.shape[1]
    for which in range(2):

        @pl.when(at_ref[CORE] == which)
        def _():
            for k in range(SIDE):
                block = sides[(k // 2 + which) % 2][k % 2]
                for i in range(SIDE):
                    held[SIDE * k + i] = block[i * rows : (i + 1) * rows]

    for t, out in enumerate(outs):
        for q in range(SIDE):
            out[q] = held[at_ref[FIRST_OUT + t] + q * at_ref[STRIDE]]


def first_parts(table, mine, other):
    _, block, half = mine.shape
    rows = block // SIDE
    return in_vmem(
        first_kernel, "first_parts",
        [jax.ShapeDtypeStruct((SIDE, rows, half), jnp.bfloat16)] * SIDE, mine, other,
        scratch=[pltpu.VMEM((SIDE**2, rows, half), jnp.bfloat16)], table=table,
    )


def second_kernel(at_ref, *refs):
    parts, outs = refs[:4], refs[4:]
    for t, out in enumerate(outs):
        out[...] = total_of(parts, at_ref[SECOND_OUT + t]).astype(out.dtype)


def second_parts(table, parts):
    shape = parts[0].shape[1:]
    return in_vmem(
        second_kernel, "second_parts",
        [jax.ShapeDtypeStruct(shape, jnp.float32)]
        + [jax.ShapeDtypeStruct(shape, jnp.bfloat16)] * (SIDE - 1),
        *parts, table=table,
    )


def cross(array, distance, diagonal_core):
    pairs = []
    for i in range(SIDE):
        for j in range(SIDE):
            for k in range(SIDE):
                for core in range(2):
                    to = [i, j, k]
                    for axis in (0, 1) if core == diagonal_core else (2,):
                        to[axis] = (to[axis] + distance) % SIDE
                    flat = [((p * SIDE + q) * SIDE + r) * 2 + core for p, q, r in ((i, j, k), to)]
                    pairs.append(tuple(flat))
    return lax.ppermute(array, ("y", "z", "x", "core"), pairs)


def stage_kernel(weight_ref, projector_ref, weight_out, projector_out, sems):
    copies = [
        pltpu.make_async_copy(weight_ref, weight_out, sems.at[0]),
        pltpu.make_async_copy(projector_ref, projector_out, sems.at[1]),
    ]
    for copy in copies:
        copy.start()
    for copy in copies:
        copy.wait()


def stage(weight, projector):
    return pl.pallas_call(
        stage_kernel,
        in_specs=[ANY] * 2,
        out_specs=[VMEM] * 2,
        out_shape=[
            jax.ShapeDtypeStruct(weight.shape, weight.dtype),
            jax.ShapeDtypeStruct(projector.shape, projector.dtype),
        ],
        scratch_shapes=[pltpu.SemaphoreType.DMA((2,))],
        compiler_params=pltpu.CompilerParams(vmem_limit_bytes=16 << 20),
        name="stage",
    )(weight, projector)


def update_kernel(
    at_ref, own_ref, own_far_ref, other_ref, other_far_ref, projector_ref, weight_ref, out_ref,
    quarters, direction,
):
    i = pl.program_id(0)
    rows, half = own_ref.shape
    depth = out_ref.shape[1]

    @pl.when(i == 0)
    def _():
        for which in range(2):

            @pl.when(at_ref[CORE] == which)
            def _():
                for near, far, place in (
                    (own_ref, own_far_ref, which), (other_ref, other_far_ref, 1 - which)
                ):
                    columns = pl.ds(place * half, half)
                    quarters[at_ref[QUARTER], :, columns] = near[...]
                    for t in range(1, SIDE):
                        quarters[at_ref[QUARTER + t], :, columns] = far[t - 1]

        for q in range(SIDE):
            direction[q * rows : (q + 1) * rows] = quarters[q]

    place = pl.ds(pl.multiple_of(at_ref[PLACE + i] * depth, depth), depth)
    delta = lax.dot_general(
        direction[...],
        projector_ref[pl.ds(pl.multiple_of(i * depth, depth), depth)],
        (((1,), (1,)), ((), ())),
        preferred_element_type=jnp.float32,
    )
    out_ref[...] = (weight_ref[:, place].astype(jnp.float32) - step_size * delta).astype(
        out_ref.dtype
    )


def update(table, own, own_far, other, other_far, projector, weight):
    block, width = weight.shape
    rank = projector.shape[1]
    rows = own.shape[0]
    parts = 8
    return pl.pallas_call(
        update_kernel,
        grid_spec=pltpu.PrefetchScalarGridSpec(
            num_scalar_prefetch=1,
            grid=(parts,),
            in_specs=[VMEM] * 6,
            out_specs=pl.BlockSpec((block, width // parts), lambda i, at: (0, at[PLACE + i])),
            scratch_shapes=[
                pltpu.VMEM((SIDE, rows, rank), own.dtype),
                pltpu.VMEM((block, rank), own.dtype),
            ],
        ),
        out_shape=jax.ShapeDtypeStruct(weight.shape, weight.dtype),
        compiler_params=pltpu.CompilerParams(vmem_limit_bytes=20 << 20),
        name="update",
    )(table, own, own_far, other, other_far, projector, weight)


def exchange(array, distance):
    pairs = []
    for i in range(SIDE):
        for j in range(SIDE):
            pairs.append(((SIDE * i + j) * 2, (SIDE * ((i - distance) % SIDE) + j) * 2))
            pairs.append(((SIDE * i + j) * 2 + 1, (SIDE * i + (j + distance) % SIDE) * 2 + 1))
    return lax.ppermute(array, ("y", "z", "core"), pairs)


def on_device(activations, out_grad, projector, weight, first_moment, second_moment):
    y, z, x, core = (lax.axis_index(name) for name in ("y", "z", "x", "core"))
    depth, rank = projector.shape
    half = rank // 2
    scale = 1.0 / math.sqrt(activations.shape[0] * SIDE**3 * 2)

    def own(array, axis):
        return lax.dynamic_slice_in_dim(array, core * half, half, axis)

    def others(array, axis):
        return lax.dynamic_slice_in_dim(array, (1 - core) * half, half, axis)

    def swap(array):
        return lax.ppermute(array, "core", SWAP)

    firsts = [
        SIDE * j + lax.rem(z - y + 2 * core + j + SIDE + distance, SIDE)
        for distance in DISTANCES
        for j in range(2)
    ]
    places = [
        2 * lax.rem(x + r, SIDE) + which for r in (0, 1, 3, 2) for which in (core, 1 - core)
    ]
    block_at = [lax.rem(y + t, SIDE) for t in range(SIDE)]
    quarter_at = [lax.rem(x + t, SIDE) for t in range(SIDE)]
    first_out = [jnp.where(core == 0, SIDE * p, q) for p, q in zip(block_at, quarter_at, strict=True)]
    second_out = [jnp.where(core == 0, q, p) for p, q in zip(block_at, quarter_at, strict=True)]
    table = jnp.stack([core, *firsts, *places, *first_out, 1 + 3 * core, *second_out, *quarter_at]).astype(jnp.int32)
    table, projector, out_grad = lax.optimization_barrier((table, projector, out_grad))

    def product(place, part):
        return jnp.dot(
            lax.dynamic_slice_in_dim(activations, places[place] * depth, depth, 1),
            part,
            preferred_element_type=jnp.float32,
        )

    near = [hop(projector, "x", -1), hop(projector, "x", 1)]
    here = [projector, swap(projector)]
    other = swap(out_grad)
    total = product(0, here[0]) + product(1, here[1])
    near, total = lax.optimization_barrier((near, total))
    half_depth = depth // 2
    far = [hop(near[1][:half_depth], "x", 1), hop(near[0][half_depth:], "x", -1)]
    near = [near[0], swap(near[0]), near[1], swap(near[1])]
    for place, part in enumerate(near):
        total += product(2 + place, part)
    far, total = lax.optimization_barrier((far, total))
    far = [jnp.concatenate(far, axis=0)]
    far += [swap(far[0])]
    for place, part in enumerate(far):
        total += product(6 + place, part)
    reduced = total.astype(jnp.bfloat16)
    reduced_other = swap(reduced)

    first_moment, second_moment, _ = lax.optimization_barrier(
        (first_moment, second_moment, near[0])
    )
    moments = jnp.stack([first_moment, second_moment])
    rows = moments.shape[1]
    moments_other = swap(others(moments, 2))
    moments_own = own(moments, 2)
    moments = jnp.where(
        core == 0,
        jnp.concatenate([moments_own, moments_other], axis=1),
        jnp.concatenate([moments_other, moments_own], axis=1),
    )
    weight, _ = lax.optimization_barrier((weight, far[0]))
    weight_all = lax.all_gather(weight, ("x", "core"), axis=0, tiled=True)

    sums = []
    for number, distance in enumerate(DISTANCES):
        (part,) = diagonal_grad((number,), table, out_grad, other, reduced, reduced_other)
        sums.append(exchange(part, distance) if distance else part)
    parts = [*here, *near, *far]
    sums[3], parts = lax.optimization_barrier((sums[3], parts))
    projector_all = jnp.concatenate(parts, axis=0)
    sums[0], projector_all, weight_all, moments = lax.optimization_barrier(
        (sums[0], projector_all, weight_all, moments)
    )
    mine, other = sum_halves(table, sums)
    sums = first_parts(table, mine, swap(other))
    sums = [sums[0], *(cross(sums[t], t, 0) for t in (2, 1, 3))]
    sums = second_parts(table, sums)
    sums = [sums[0], *(cross(sums[t], t, 1) for t in (2, 1, 3))]
    grad = sum(part.astype(jnp.float32) for part in sums)
    grad = grad * scale

    new_first = beta_first * moments[0] + (1.0 - beta_first) * grad
    new_second = beta_second * moments[1] + (1.0 - beta_second) * grad * grad
    direction = (
        new_first / correct_first / (jnp.sqrt(new_second / correct_second) + epsilon)
    ).astype(jnp.bfloat16)

    direction, projector_all, weight_all = lax.optimization_barrier(
        (direction, projector_all, weight_all)
    )
    weight_all, projector_all = stage(weight_all.T, projector_all)
    far = [hop(direction, "x", -t) for t in (2, 1, 3)]
    other = swap(direction)
    far, weight_all, projector_all = lax.optimization_barrier((far, weight_all, projector_all))
    far = jnp.stack([far[1], far[0], far[2]])
    other_far = swap(far)
    new_weight = update(table, direction, far, other, other_far, projector_all, weight_all).T
    new_first, new_second, _ = lax.optimization_barrier((new_first, new_second, far))

    news = jnp.stack([new_first, new_second])
    kept = lax.dynamic_slice_in_dim(news, core * rows, rows, 1)
    came = swap(lax.dynamic_slice_in_dim(news, (1 - core) * rows, rows, 1))
    news = jnp.where(
        core == 0,
        jnp.concatenate([kept, came], axis=2),
        jnp.concatenate([came, kept], axis=2),
    )
    return (new_weight, news[0], news[1])


def solution(mesh):
    grid = Mesh(mesh.devices.reshape(SIDE, SIDE, SIDE, 2), ("y", "z", "x", "core"))
    everywhere, group = ("y", "z", "x", "core"), ("x", "core")
    in_specs = (
        P(everywhere, None),
        P(everywhere, None),
        P(group, None),
        P(group, ("y", "z")),
        P(everywhere, None),
        P(everywhere, None),
    )
    out_specs = (P(None, ("y", "z")), P(everywhere, None), P(everywhere, None))
    return jax.shard_map(
        on_device, mesh=grid, in_specs=in_specs, out_specs=out_specs, check_vma=False
    )
```

```python
import functools
import math

import jax
import jax.numpy as jnp
from jax import lax
from jax.experimental import pallas as pl
from jax.experimental.pallas import tpu as pltpu
from jax.sharding import Mesh
from jax.sharding import PartitionSpec as P

beta_first = 0.9
beta_second = 0.95
correct_first = 1.0 - 0.9**4
correct_second = 1.0 - 0.95**4
epsilon = 1e-08
step_size = 4.0

SIDE = 4
SWAP = ((0, 1), (1, 0))
CORE, FIRST, PLACE, FIRST_OUT, STRIDE, SECOND_OUT, QUARTER = 0, 1, 9, 17, 21, 22, 26
DISTANCES = (2, 3, 1, 0)


def hop(array, axis, distance):
    return lax.ppermute(array, axis, [(i, (i + distance) % SIDE) for i in range(SIDE)])


VMEM = pl.BlockSpec(memory_space=pltpu.VMEM)
SMEM = pl.BlockSpec(memory_space=pltpu.SMEM)


def in_vmem(kernel, name, out_shape, *operands, scratch=(), limit=16, table=None):
    first = [] if table is None else [SMEM]
    operands = operands if table is None else (table, *operands)
    return pl.pallas_call(
        kernel,
        in_specs=first + [VMEM] * (len(operands) - len(first)),
        out_specs=jax.tree.map(lambda _: VMEM, out_shape),
        out_shape=out_shape,
        scratch_shapes=list(scratch),
        compiler_params=pltpu.CompilerParams(vmem_limit_bytes=limit << 20),
        name=name,
    )(*operands)


ANY = pl.BlockSpec(memory_space=pl.ANY)


def diagonal_kernel(
    numbers, at_ref, mine_ref, other_ref, reduced_ref, reduced_other_ref, *refs
):
    outs, (windows, reduced, held, sems) = refs[:-4], refs[-4:]
    contract = (((0,), (0,)), ((), ()))
    tokens, hidden = mine_ref.shape
    hidden //= 2
    window = held.shape[0]
    blocks, block, _ = outs[0].shape
    offset = pl.multiple_of(at_ref[CORE] * hidden, 128)
    skips, copies = [], []
    for i, (n, j) in enumerate((n, j) for n in numbers for j in range(blocks)):
        first = at_ref[FIRST + blocks * n + j] * block
        start = pl.multiple_of(jnp.minimum(first // 128 * 128, hidden - window), 128)
        skips.append(pl.multiple_of(first - start, 16))
        copies.append(
            [
                pltpu.make_async_copy(
                    ref.at[:, pl.ds(pl.multiple_of(start + offset, 128), window)],
                    windows.at[i, pl.ds(side * tokens, tokens)],
                    sems.at[i, side],
                )
                for side, ref in enumerate((mine_ref, other_ref))
            ]
        )
        for copy in copies[-1]:
            copy.start()
    reduced[:tokens] = reduced_ref[...]
    reduced[tokens:] = reduced_other_ref[...]
    for i, skip in enumerate(skips):
        for copy in copies[i]:
            copy.wait()
        total = lax.dot_general(
            windows[i], reduced[...], contract, preferred_element_type=jnp.float32
        )
        held[...] = total.astype(held.dtype)
        outs[i // blocks][i % blocks] = held[pl.ds(skip, block)]


def diagonal_grad(numbers, table, mine, other, reduced, reduced_other):
    tokens, hidden = mine.shape
    columns = reduced.shape[1]
    out = jax.ShapeDtypeStruct((2, hidden // SIDE**2, columns), jnp.bfloat16)
    window = 896
    count = 2 * len(numbers)
    return pl.pallas_call(
        functools.partial(diagonal_kernel, numbers),
        in_specs=[SMEM] + [ANY] * 2 + [VMEM] * 2,
        out_specs=[VMEM] * len(numbers),
        out_shape=[out] * len(numbers),
        scratch_shapes=[
            pltpu.VMEM((count, 2 * tokens, window), jnp.bfloat16),
            pltpu.VMEM((2 * tokens, columns), jnp.bfloat16),
            pltpu.VMEM((window, columns), jnp.bfloat16),
            pltpu.SemaphoreType.DMA((count, 2)),
        ],
        cost_estimate=pl.CostEstimate(
            flops=4 * count * tokens * window * columns,
            bytes_accessed=4 * count * tokens * window,
            transcendentals=0,
        ),
        compiler_params=pltpu.CompilerParams(vmem_limit_bytes=50 << 20),
        name="diagonal_grad",
    )(table, mine, other, reduced, reduced_other)


def total_of(parts, *index):
    total = parts[0][index].astype(jnp.float32)
    for part in parts[1:]:
        total += part[index].astype(jnp.float32)
    return total


def half_kernel(at_ref, *refs):
    parts, out = refs[:4], refs[4]
    for j in range(out.shape[0]):
        out[j] = total_of(parts, j).astype(out.dtype)


def sum_half(table, parts, mine):
    blocks, block, columns = parts[0].shape
    half = pl.BlockSpec(
        (blocks, block, columns // 2),
        (lambda i, at: (0, 0, at[CORE])) if mine else (lambda i, at: (0, 0, 1 - at[CORE])),
    )
    return pl.pallas_call(
        half_kernel,
        grid_spec=pltpu.PrefetchScalarGridSpec(
            num_scalar_prefetch=1, grid=(1,), in_specs=[half] * len(parts), out_specs=VMEM
        ),
        out_shape=jax.ShapeDtypeStruct((blocks, block, columns // 2), jnp.bfloat16),
        compiler_params=pltpu.CompilerParams(vmem_limit_bytes=20 << 20),
        name="sum_half",
    )(table, *parts)


def first_kernel(at_ref, *refs):
    sides, outs, held = refs[:2], refs[2:6], refs[6]
    rows = held.shape[1]
    for which in range(2):

        @pl.when(at_ref[CORE] == which)
        def _():
            for k in range(SIDE):
                block = sides[(k // 2 + which) % 2][k % 2]
                for i in range(SIDE):
                    held[SIDE * k + i] = block[i * rows : (i + 1) * rows]

    for t, out in enumerate(outs):
        for q in range(SIDE):
            out[q] = held[at_ref[FIRST_OUT + t] + q * at_ref[STRIDE]]


def first_parts(table, mine, other):
    _, block, half = mine.shape
    rows = block // SIDE
    return in_vmem(
        first_kernel, "first_parts",
        [jax.ShapeDtypeStruct((SIDE, rows, half), jnp.bfloat16)] * SIDE, mine, other,
        scratch=[pltpu.VMEM((SIDE**2, rows, half), jnp.bfloat16)], table=table,
    )


def second_kernel(at_ref, *refs):
    parts, outs = refs[:4], refs[4:]
    for t, out in enumerate(outs):
        out[...] = total_of(parts, at_ref[SECOND_OUT + t]).astype(out.dtype)


def second_parts(table, parts):
    shape = parts[0].shape[1:]
    return in_vmem(
        second_kernel, "second_parts",
        [jax.ShapeDtypeStruct(shape, jnp.float32)]
        + [jax.ShapeDtypeStruct(shape, jnp.bfloat16)] * (SIDE - 1),
        *parts, table=table,
    )


def cross(array, distance, diagonal_core):
    pairs = []
    for i in range(SIDE):
        for j in range(SIDE):
            for k in range(SIDE):
                for core in range(2):
                    to = [i, j, k]
                    for axis in (0, 1) if core == diagonal_core else (2,):
                        to[axis] = (to[axis] + distance) % SIDE
                    flat = [((p * SIDE + q) * SIDE + r) * 2 + core for p, q, r in ((i, j, k), to)]
                    pairs.append(tuple(flat))
    return lax.ppermute(array, ("y", "z", "x", "core"), pairs)


def stage_kernel(weight_ref, projector_ref, weight_out, projector_out, sems):
    copies = [
        pltpu.make_async_copy(weight_ref, weight_out, sems.at[0]),
        pltpu.make_async_copy(projector_ref, projector_out, sems.at[1]),
    ]
    for copy in copies:
        copy.start()
    for copy in copies:
        copy.wait()


def stage(weight, projector):
    return pl.pallas_call(
        stage_kernel,
        in_specs=[ANY] * 2,
        out_specs=[VMEM] * 2,
        out_shape=[
            jax.ShapeDtypeStruct(weight.shape, weight.dtype),
            jax.ShapeDtypeStruct(projector.shape, projector.dtype),
        ],
        scratch_shapes=[pltpu.SemaphoreType.DMA((2,))],
        compiler_params=pltpu.CompilerParams(vmem_limit_bytes=16 << 20),
        name="stage",
    )(weight, projector)


def update_kernel(
    at_ref, own_ref, own_far_ref, other_ref, other_far_ref, projector_ref, weight_ref, out_ref,
    quarters, direction,
):
    i = pl.program_id(0)
    rows, half = own_ref.shape
    depth = out_ref.shape[1]

    @pl.when(i == 0)
    def _():
        for which in range(2):

            @pl.when(at_ref[CORE] == which)
            def _():
                for near, far, place in (
                    (own_ref, own_far_ref, which), (other_ref, other_far_ref, 1 - which)
                ):
                    columns = pl.ds(place * half, half)
                    quarters[at_ref[QUARTER], :, columns] = near[...]
                    for t in range(1, SIDE):
                        quarters[at_ref[QUARTER + t], :, columns] = far[t - 1]

        for q in range(SIDE):
            direction[q * rows : (q + 1) * rows] = quarters[q]

    place = pl.ds(pl.multiple_of(at_ref[PLACE + i] * depth, depth), depth)
    delta = lax.dot_general(
        direction[...],
        projector_ref[pl.ds(pl.multiple_of(i * depth, depth), depth)],
        (((1,), (1,)), ((), ())),
        preferred_element_type=jnp.float32,
    )
    out_ref[...] = (weight_ref[:, place].astype(jnp.float32) - step_size * delta).astype(
        out_ref.dtype
    )


def update(table, own, own_far, other, other_far, projector, weight):
    block, width = weight.shape
    rank = projector.shape[1]
    rows = own.shape[0]
    parts = 8
    return pl.pallas_call(
        update_kernel,
        grid_spec=pltpu.PrefetchScalarGridSpec(
            num_scalar_prefetch=1,
            grid=(parts,),
            in_specs=[VMEM] * 6,
            out_specs=pl.BlockSpec((block, width // parts), lambda i, at: (0, at[PLACE + i])),
            scratch_shapes=[
                pltpu.VMEM((SIDE, rows, rank), own.dtype),
                pltpu.VMEM((block, rank), own.dtype),
            ],
        ),
        out_shape=jax.ShapeDtypeStruct(weight.shape, weight.dtype),
        compiler_params=pltpu.CompilerParams(vmem_limit_bytes=20 << 20),
        name="update",
    )(table, own, own_far, other, other_far, projector, weight)


def exchange(array, distance):
    pairs = []
    for i in range(SIDE):
        for j in range(SIDE):
            pairs.append(((SIDE * i + j) * 2, (SIDE * ((i - distance) % SIDE) + j) * 2))
            pairs.append(((SIDE * i + j) * 2 + 1, (SIDE * i + (j + distance) % SIDE) * 2 + 1))
    return lax.ppermute(array, ("y", "z", "core"), pairs)


def on_device(activations, out_grad, projector, weight, first_moment, second_moment):
    y, z, x, core = (lax.axis_index(name) for name in ("y", "z", "x", "core"))
    depth, rank = projector.shape
    half = rank // 2
    scale = 1.0 / math.sqrt(activations.shape[0] * SIDE**3 * 2)

    def own(array, axis):
        return lax.dynamic_slice_in_dim(array, core * half, half, axis)

    def others(array, axis):
        return lax.dynamic_slice_in_dim(array, (1 - core) * half, half, axis)

    def swap(array):
        return lax.ppermute(array, "core", SWAP)

    firsts = [
        SIDE * j + lax.rem(z - y + 2 * core + j + SIDE + distance, SIDE)
        for distance in DISTANCES
        for j in range(2)
    ]
    places = [
        2 * lax.rem(x + r, SIDE) + which for r in (0, 1, 3, 2) for which in (core, 1 - core)
    ]
    block_at = [lax.rem(y + t, SIDE) for t in range(SIDE)]
    quarter_at = [lax.rem(x + t, SIDE) for t in range(SIDE)]
    first_out = [jnp.where(core == 0, SIDE * p, q) for p, q in zip(block_at, quarter_at, strict=True)]
    second_out = [jnp.where(core == 0, q, p) for p, q in zip(block_at, quarter_at, strict=True)]
    table = jnp.stack([core, *firsts, *places, *first_out, 1 + 3 * core, *second_out, *quarter_at]).astype(jnp.int32)
    table, projector, out_grad = lax.optimization_barrier((table, projector, out_grad))

    def columns_of(place):
        return lax.dynamic_slice_in_dim(activations, places[place] * depth, depth, 1)

    def product(place, part):
        return jnp.dot(columns_of(place), part, preferred_element_type=jnp.float32)

    near = [hop(projector, "x", -1), hop(projector, "x", 1)]
    here = [projector, swap(projector)]
    other = swap(out_grad)
    total = product(0, here[0]) + product(1, here[1])
    near, total = lax.optimization_barrier((near, total))
    half_depth = depth // 2
    far = [hop(near[1][:half_depth], "x", 1), hop(near[0][half_depth:], "x", -1)]
    near = [near[0], swap(near[0]), near[1], swap(near[1])]
    for place, part in enumerate(near):
        total += product(2 + place, part)
    last = [columns_of(6), columns_of(7)]
    far, total, last = lax.optimization_barrier((far, total, last))
    far = [jnp.concatenate(far, axis=0)]
    far += [swap(far[0])]
    for columns, part in zip(last, far, strict=True):
        total += jnp.dot(columns, part, preferred_element_type=jnp.float32)
    reduced = total.astype(jnp.bfloat16)
    reduced_other = swap(reduced)

    first_moment, second_moment, _ = lax.optimization_barrier(
        (first_moment, second_moment, near[0])
    )
    moments = jnp.stack([first_moment, second_moment])
    rows = moments.shape[1]
    moments_other = swap(others(moments, 2))
    moments_own = own(moments, 2)
    moments = jnp.where(
        core == 0,
        jnp.concatenate([moments_own, moments_other], axis=1),
        jnp.concatenate([moments_other, moments_own], axis=1),
    )
    weight, _ = lax.optimization_barrier((weight, far[0]))
    weight_all = lax.all_gather(weight, ("x", "core"), axis=0, tiled=True)

    sums = []
    for number, distance in enumerate(DISTANCES):
        (part,) = diagonal_grad((number,), table, out_grad, other, reduced, reduced_other)
        sums.append(exchange(part, distance) if distance else part)
    parts = [*here, *near, *far]
    sums[3], parts = lax.optimization_barrier((sums[3], parts))
    projector_all = jnp.concatenate(parts, axis=0)
    sums[0], projector_all, weight_all, moments = lax.optimization_barrier(
        (sums[0], projector_all, weight_all, moments)
    )
    other = sum_half(table, sums, False)
    sums[0], other = lax.optimization_barrier((sums[0], other))
    mine = sum_half(table, sums, True)
    sums = first_parts(table, mine, swap(other))
    sums = [sums[0], *(cross(sums[t], t, 0) for t in (2, 1, 3))]
    sums = second_parts(table, sums)
    sums = [sums[0], *(cross(sums[t], t, 1) for t in (2, 1, 3))]
    grad = sum(part.astype(jnp.float32) for part in sums)
    grad = grad * scale

    new_first = beta_first * moments[0] + (1.0 - beta_first) * grad
    new_second = beta_second * moments[1] + (1.0 - beta_second) * grad * grad
    direction = (
        new_first / correct_first / (jnp.sqrt(new_second / correct_second) + epsilon)
    ).astype(jnp.bfloat16)

    direction, projector_all, weight_all = lax.optimization_barrier(
        (direction, projector_all, weight_all)
    )
    weight_all, projector_all = stage(weight_all.T, projector_all)
    far = [hop(direction, "x", -t) for t in (2, 1, 3)]
    other = swap(direction)
    far, weight_all, projector_all = lax.optimization_barrier((far, weight_all, projector_all))
    far = jnp.stack([far[1], far[0], far[2]])
    other_far = swap(far)
    new_weight = update(table, direction, far, other, other_far, projector_all, weight_all).T
    new_first, new_second, _ = lax.optimization_barrier((new_first, new_second, far))

    news = jnp.stack([new_first, new_second])
    kept = lax.dynamic_slice_in_dim(news, core * rows, rows, 1)
    came = swap(lax.dynamic_slice_in_dim(news, (1 - core) * rows, rows, 1))
    news = jnp.where(
        core == 0,
        jnp.concatenate([kept, came], axis=2),
        jnp.concatenate([came, kept], axis=2),
    )
    return (new_weight, news[0], news[1])


def solution(mesh):
    grid = Mesh(mesh.devices.reshape(SIDE, SIDE, SIDE, 2), ("y", "z", "x", "core"))
    everywhere, group = ("y", "z", "x", "core"), ("x", "core")
    in_specs = (
        P(everywhere, None),
        P(everywhere, None),
        P(group, None),
        P(group, ("y", "z")),
        P(everywhere, None),
        P(everywhere, None),
    )
    out_specs = (P(None, ("y", "z")), P(everywhere, None), P(everywhere, None))
    return jax.shard_map(
        on_device, mesh=grid, in_specs=in_specs, out_specs=out_specs, check_vma=False
    )
```

```python
import functools
import math

import jax
import jax.numpy as jnp
from jax import lax
from jax.experimental import pallas as pl
from jax.experimental.pallas import tpu as pltpu
from jax.sharding import Mesh
from jax.sharding import PartitionSpec as P

beta_first = 0.9
beta_second = 0.95
correct_first = 1.0 - 0.9**4
correct_second = 1.0 - 0.95**4
epsilon = 1e-08
step_size = 4.0

SIDE = 4
SWAP = ((0, 1), (1, 0))
CORE, FIRST, PLACE, FIRST_OUT, STRIDE, SECOND_OUT, QUARTER = 0, 1, 9, 17, 21, 22, 26
DISTANCES = (2, 3, 1, 0)


def hop(array, axis, distance):
    return lax.ppermute(array, axis, [(i, (i + distance) % SIDE) for i in range(SIDE)])


VMEM = pl.BlockSpec(memory_space=pltpu.VMEM)
SMEM = pl.BlockSpec(memory_space=pltpu.SMEM)


def in_vmem(kernel, name, out_shape, *operands, scratch=(), limit=16, table=None):
    first = [] if table is None else [SMEM]
    operands = operands if table is None else (table, *operands)
    return pl.pallas_call(
        kernel,
        in_specs=first + [VMEM] * (len(operands) - len(first)),
        out_specs=jax.tree.map(lambda _: VMEM, out_shape),
        out_shape=out_shape,
        scratch_shapes=list(scratch),
        compiler_params=pltpu.CompilerParams(vmem_limit_bytes=limit << 20),
        name=name,
    )(*operands)


ANY = pl.BlockSpec(memory_space=pl.ANY)


def diagonal_kernel(
    pairs, at_ref, mine_ref, other_ref, reduced_ref, reduced_other_ref, *refs
):
    out_ref, windows, reduced, held, sems = refs
    contract = (((0,), (0,)), ((), ()))
    tokens, hidden = mine_ref.shape
    hidden //= 2
    window = held.shape[0]
    block = out_ref.shape[1]
    offset = pl.multiple_of(at_ref[CORE] * hidden, 128)
    skips, copies = [], []
    for i, (n, j) in enumerate(pairs):
        first = at_ref[FIRST + 2 * n + j] * block
        start = pl.multiple_of(jnp.minimum(first // 128 * 128, hidden - window), 128)
        skips.append(pl.multiple_of(first - start, 16))
        copies.append(
            [
                pltpu.make_async_copy(
                    ref.at[:, pl.ds(pl.multiple_of(start + offset, 128), window)],
                    windows.at[i, pl.ds(side * tokens, tokens)],
                    sems.at[i, side],
                )
                for side, ref in enumerate((mine_ref, other_ref))
            ]
        )
        for copy in copies[-1]:
            copy.start()
    reduced[:tokens] = reduced_ref[...]
    reduced[tokens:] = reduced_other_ref[...]
    for i, skip in enumerate(skips):
        for copy in copies[i]:
            copy.wait()
        total = lax.dot_general(
            windows[i], reduced[...], contract, preferred_element_type=jnp.float32
        )
        held[...] = total.astype(held.dtype)
        out_ref[i] = held[pl.ds(skip, block)]


def diagonal_grad(pairs, table, mine, other, reduced, reduced_other):
    tokens, hidden = mine.shape
    columns = reduced.shape[1]
    out = jax.ShapeDtypeStruct((len(pairs), hidden // SIDE**2, columns), jnp.bfloat16)
    window = 896
    count = len(pairs)
    return pl.pallas_call(
        functools.partial(diagonal_kernel, pairs),
        in_specs=[SMEM] + [ANY] * 2 + [VMEM] * 2,
        out_specs=VMEM,
        out_shape=out,
        scratch_shapes=[
            pltpu.VMEM((count, 2 * tokens, window), jnp.bfloat16),
            pltpu.VMEM((2 * tokens, columns), jnp.bfloat16),
            pltpu.VMEM((window, columns), jnp.bfloat16),
            pltpu.SemaphoreType.DMA((count, 2)),
        ],
        cost_estimate=pl.CostEstimate(
            flops=4 * count * tokens * window * columns,
            bytes_accessed=4 * count * tokens * window,
            transcendentals=0,
        ),
        compiler_params=pltpu.CompilerParams(vmem_limit_bytes=50 << 20),
        name="diagonal_grad",
    )(table, mine, other, reduced, reduced_other)


def total_of(parts, *index):
    total = parts[0][index].astype(jnp.float32)
    for part in parts[1:]:
        total += part[index].astype(jnp.float32)
    return total


def half_kernel(at_ref, *refs):
    parts, out = refs[:4], refs[4]
    for j in range(out.shape[0]):
        out[j] = total_of(parts, j).astype(out.dtype)


def sum_half(table, parts, mine):
    blocks, block, columns = parts[0].shape
    half = pl.BlockSpec(
        (blocks, block, columns // 2),
        (lambda i, at: (0, 0, at[CORE])) if mine else (lambda i, at: (0, 0, 1 - at[CORE])),
    )
    return pl.pallas_call(
        half_kernel,
        grid_spec=pltpu.PrefetchScalarGridSpec(
            num_scalar_prefetch=1, grid=(1,), in_specs=[half] * len(parts), out_specs=VMEM
        ),
        out_shape=jax.ShapeDtypeStruct((blocks, block, columns // 2), jnp.bfloat16),
        compiler_params=pltpu.CompilerParams(vmem_limit_bytes=20 << 20),
        name="sum_half",
    )(table, *parts)


def first_kernel(at_ref, *refs):
    sides, outs, held = refs[:2], refs[2:6], refs[6]
    rows = held.shape[1]
    for which in range(2):

        @pl.when(at_ref[CORE] == which)
        def _():
            for k in range(SIDE):
                block = sides[(k // 2 + which) % 2][k % 2]
                for i in range(SIDE):
                    held[SIDE * k + i] = block[i * rows : (i + 1) * rows]

    for t, out in enumerate(outs):
        for q in range(SIDE):
            out[q] = held[at_ref[FIRST_OUT + t] + q * at_ref[STRIDE]]


def first_parts(table, mine, other):
    _, block, half = mine.shape
    rows = block // SIDE
    return in_vmem(
        first_kernel, "first_parts",
        [jax.ShapeDtypeStruct((SIDE, rows, half), jnp.bfloat16)] * SIDE, mine, other,
        scratch=[pltpu.VMEM((SIDE**2, rows, half), jnp.bfloat16)], table=table,
    )


def second_kernel(at_ref, *refs):
    parts, outs = refs[:4], refs[4:]
    for t, out in enumerate(outs):
        out[...] = total_of(parts, at_ref[SECOND_OUT + t]).astype(out.dtype)


def second_parts(table, parts):
    shape = parts[0].shape[1:]
    return in_vmem(
        second_kernel, "second_parts",
        [jax.ShapeDtypeStruct(shape, jnp.float32)]
        + [jax.ShapeDtypeStruct(shape, jnp.bfloat16)] * (SIDE - 1),
        *parts, table=table,
    )


def cross(array, distance, diagonal_core):
    pairs = []
    for i in range(SIDE):
        for j in range(SIDE):
            for k in range(SIDE):
                for core in range(2):
                    to = [i, j, k]
                    for axis in (0, 1) if core == diagonal_core else (2,):
                        to[axis] = (to[axis] + distance) % SIDE
                    flat = [((p * SIDE + q) * SIDE + r) * 2 + core for p, q, r in ((i, j, k), to)]
                    pairs.append(tuple(flat))
    return lax.ppermute(array, ("y", "z", "x", "core"), pairs)


def stage_kernel(weight_ref, projector_ref, weight_out, projector_out, sems):
    copies = [
        pltpu.make_async_copy(weight_ref, weight_out, sems.at[0]),
        pltpu.make_async_copy(projector_ref, projector_out, sems.at[1]),
    ]
    for copy in copies:
        copy.start()
    for copy in copies:
        copy.wait()


def stage(weight, projector):
    return pl.pallas_call(
        stage_kernel,
        in_specs=[ANY] * 2,
        out_specs=[VMEM] * 2,
        out_shape=[
            jax.ShapeDtypeStruct(weight.shape, weight.dtype),
            jax.ShapeDtypeStruct(projector.shape, projector.dtype),
        ],
        scratch_shapes=[pltpu.SemaphoreType.DMA((2,))],
        compiler_params=pltpu.CompilerParams(vmem_limit_bytes=16 << 20),
        name="stage",
    )(weight, projector)


def update_kernel(
    at_ref, own_ref, own_far_ref, other_ref, other_far_ref, projector_ref, weight_ref, out_ref,
    quarters, direction,
):
    i = pl.program_id(0)
    rows, half = own_ref.shape
    depth = out_ref.shape[1]

    @pl.when(i == 0)
    def _():
        for which in range(2):

            @pl.when(at_ref[CORE] == which)
            def _():
                for near, far, place in (
                    (own_ref, own_far_ref, which), (other_ref, other_far_ref, 1 - which)
                ):
                    columns = pl.ds(place * half, half)
                    quarters[at_ref[QUARTER], :, columns] = near[...]
                    for t in range(1, SIDE):
                        quarters[at_ref[QUARTER + t], :, columns] = far[t - 1]

        for q in range(SIDE):
            direction[q * rows : (q + 1) * rows] = quarters[q]

    place = pl.ds(pl.multiple_of(at_ref[PLACE + i] * depth, depth), depth)
    delta = lax.dot_general(
        direction[...],
        projector_ref[pl.ds(pl.multiple_of(i * depth, depth), depth)],
        (((1,), (1,)), ((), ())),
        preferred_element_type=jnp.float32,
    )
    out_ref[...] = (weight_ref[:, place].astype(jnp.float32) - step_size * delta).astype(
        out_ref.dtype
    )


def update(table, own, own_far, other, other_far, projector, weight):
    block, width = weight.shape
    rank = projector.shape[1]
    rows = own.shape[0]
    parts = 8
    return pl.pallas_call(
        update_kernel,
        grid_spec=pltpu.PrefetchScalarGridSpec(
            num_scalar_prefetch=1,
            grid=(parts,),
            in_specs=[VMEM] * 6,
            out_specs=pl.BlockSpec((block, width // parts), lambda i, at: (0, at[PLACE + i])),
            scratch_shapes=[
                pltpu.VMEM((SIDE, rows, rank), own.dtype),
                pltpu.VMEM((block, rank), own.dtype),
            ],
        ),
        out_shape=jax.ShapeDtypeStruct(weight.shape, weight.dtype),
        compiler_params=pltpu.CompilerParams(vmem_limit_bytes=20 << 20),
        name="update",
    )(table, own, own_far, other, other_far, projector, weight)


def exchange(array, distance):
    pairs = []
    for i in range(SIDE):
        for j in range(SIDE):
            pairs.append(((SIDE * i + j) * 2, (SIDE * ((i - distance) % SIDE) + j) * 2))
            pairs.append(((SIDE * i + j) * 2 + 1, (SIDE * i + (j + distance) % SIDE) * 2 + 1))
    return lax.ppermute(array, ("y", "z", "core"), pairs)


def on_device(activations, out_grad, projector, weight, first_moment, second_moment):
    y, z, x, core = (lax.axis_index(name) for name in ("y", "z", "x", "core"))
    depth, rank = projector.shape
    half = rank // 2
    scale = 1.0 / math.sqrt(activations.shape[0] * SIDE**3 * 2)

    def own(array, axis):
        return lax.dynamic_slice_in_dim(array, core * half, half, axis)

    def others(array, axis):
        return lax.dynamic_slice_in_dim(array, (1 - core) * half, half, axis)

    def swap(array):
        return lax.ppermute(array, "core", SWAP)

    firsts = [
        SIDE * j + lax.rem(z - y + 2 * core + j + SIDE + distance, SIDE)
        for distance in DISTANCES
        for j in range(2)
    ]
    places = [
        2 * lax.rem(x + r, SIDE) + which for r in (0, 1, 3, 2) for which in (core, 1 - core)
    ]
    block_at = [lax.rem(y + t, SIDE) for t in range(SIDE)]
    quarter_at = [lax.rem(x + t, SIDE) for t in range(SIDE)]
    first_out = [jnp.where(core == 0, SIDE * p, q) for p, q in zip(block_at, quarter_at, strict=True)]
    second_out = [jnp.where(core == 0, q, p) for p, q in zip(block_at, quarter_at, strict=True)]
    table = jnp.stack([core, *firsts, *places, *first_out, 1 + 3 * core, *second_out, *quarter_at]).astype(jnp.int32)
    table, projector, out_grad = lax.optimization_barrier((table, projector, out_grad))

    def columns_of(place):
        return lax.dynamic_slice_in_dim(activations, places[place] * depth, depth, 1)

    def product(place, part):
        return jnp.dot(columns_of(place), part, preferred_element_type=jnp.float32)

    near = [hop(projector, "x", -1), hop(projector, "x", 1)]
    here = [projector, swap(projector)]
    other = swap(out_grad)
    total = product(0, here[0]) + product(1, here[1])
    near, total = lax.optimization_barrier((near, total))
    half_depth = depth // 2
    far = [hop(near[1][:half_depth], "x", 1), hop(near[0][half_depth:], "x", -1)]
    near = [near[0], swap(near[0]), near[1], swap(near[1])]
    for place, part in enumerate(near):
        total += product(2 + place, part)
    last = [columns_of(6), columns_of(7)]
    far, total, last = lax.optimization_barrier((far, total, last))
    far = [jnp.concatenate(far, axis=0)]
    far += [swap(far[0])]
    for columns, part in zip(last, far, strict=True):
        total += jnp.dot(columns, part, preferred_element_type=jnp.float32)
    reduced = total.astype(jnp.bfloat16)
    reduced_other = swap(reduced)

    first_moment, second_moment, _ = lax.optimization_barrier(
        (first_moment, second_moment, near[0])
    )
    moments = jnp.stack([first_moment, second_moment])
    rows = moments.shape[1]
    moments_other = swap(others(moments, 2))
    moments_own = own(moments, 2)
    moments = jnp.where(
        core == 0,
        jnp.concatenate([moments_own, moments_other], axis=1),
        jnp.concatenate([moments_other, moments_own], axis=1),
    )
    weight, _ = lax.optimization_barrier((weight, far[0]))
    weight_all = lax.all_gather(weight, ("x", "core"), axis=0, tiled=True)

    sums = []
    for number, distance in enumerate(DISTANCES):
        pairs = [(number, 0), (number, 1)]
        arrived = []
        for some in ([pairs[:1], pairs[1:]] if number == 0 else [pairs]):
            part = diagonal_grad(some, table, out_grad, other, reduced, reduced_other)
            arrived.append(exchange(part, distance) if distance else part)
        sums.append(jnp.concatenate(arrived, axis=0))
    parts = [*here, *near, *far]
    sums[3], parts = lax.optimization_barrier((sums[3], parts))
    projector_all = jnp.concatenate(parts, axis=0)
    sums[0], projector_all, weight_all, moments = lax.optimization_barrier(
        (sums[0], projector_all, weight_all, moments)
    )
    other = sum_half(table, sums, False)
    sums[0], other = lax.optimization_barrier((sums[0], other))
    mine = sum_half(table, sums, True)
    sums = first_parts(table, mine, swap(other))
    sums = [sums[0], *(cross(sums[t], t, 0) for t in (2, 1, 3))]
    sums = second_parts(table, sums)
    sums = [sums[0], *(cross(sums[t], t, 1) for t in (2, 1, 3))]
    grad = sum(part.astype(jnp.float32) for part in sums)
    grad = grad * scale

    new_first = beta_first * moments[0] + (1.0 - beta_first) * grad
    new_second = beta_second * moments[1] + (1.0 - beta_second) * grad * grad
    direction = (
        new_first / correct_first / (jnp.sqrt(new_second / correct_second) + epsilon)
    ).astype(jnp.bfloat16)

    direction, projector_all, weight_all = lax.optimization_barrier(
        (direction, projector_all, weight_all)
    )
    weight_all, projector_all = stage(weight_all.T, projector_all)
    far = [hop(direction, "x", -t) for t in (2, 1, 3)]
    other = swap(direction)
    far, weight_all, projector_all = lax.optimization_barrier((far, weight_all, projector_all))
    far = jnp.stack([far[1], far[0], far[2]])
    other_far = swap(far)
    new_weight = update(table, direction, far, other, other_far, projector_all, weight_all).T
    new_first, new_second, _ = lax.optimization_barrier((new_first, new_second, far))

    news = jnp.stack([new_first, new_second])
    kept = lax.dynamic_slice_in_dim(news, core * rows, rows, 1)
    came = swap(lax.dynamic_slice_in_dim(news, (1 - core) * rows, rows, 1))
    news = jnp.where(
        core == 0,
        jnp.concatenate([kept, came], axis=2),
        jnp.concatenate([came, kept], axis=2),
    )
    return (new_weight, news[0], news[1])


def solution(mesh):
    grid = Mesh(mesh.devices.reshape(SIDE, SIDE, SIDE, 2), ("y", "z", "x", "core"))
    everywhere, group = ("y", "z", "x", "core"), ("x", "core")
    in_specs = (
        P(everywhere, None),
        P(everywhere, None),
        P(group, None),
        P(group, ("y", "z")),
        P(everywhere, None),
        P(everywhere, None),
    )
    out_specs = (P(None, ("y", "z")), P(everywhere, None), P(everywhere, None))
    return jax.shard_map(
        on_device, mesh=grid, in_specs=in_specs, out_specs=out_specs, check_vma=False
    )
```

```python
import functools
import math

import jax
import jax.numpy as jnp
from jax import lax
from jax.experimental import pallas as pl
from jax.experimental.pallas import tpu as pltpu
from jax.sharding import Mesh
from jax.sharding import PartitionSpec as P

beta_first = 0.9
beta_second = 0.95
correct_first = 1.0 - 0.9**4
correct_second = 1.0 - 0.95**4
epsilon = 1e-08
step_size = 4.0

SIDE = 4
SWAP = ((0, 1), (1, 0))
CORE, FIRST, PLACE, FIRST_OUT, STRIDE, SECOND_OUT, QUARTER = 0, 1, 9, 17, 21, 22, 26
DISTANCES = (2, 3, 1, 0)


def hop(array, axis, distance):
    return lax.ppermute(array, axis, [(i, (i + distance) % SIDE) for i in range(SIDE)])


VMEM = pl.BlockSpec(memory_space=pltpu.VMEM)
SMEM = pl.BlockSpec(memory_space=pltpu.SMEM)


def in_vmem(kernel, name, out_shape, *operands, scratch=(), limit=16, table=None):
    first = [] if table is None else [SMEM]
    operands = operands if table is None else (table, *operands)
    return pl.pallas_call(
        kernel,
        in_specs=first + [VMEM] * (len(operands) - len(first)),
        out_specs=jax.tree.map(lambda _: VMEM, out_shape),
        out_shape=out_shape,
        scratch_shapes=list(scratch),
        compiler_params=pltpu.CompilerParams(vmem_limit_bytes=limit << 20),
        name=name,
    )(*operands)


ANY = pl.BlockSpec(memory_space=pl.ANY)


def diagonal_kernel(
    numbers, at_ref, mine_ref, other_ref, reduced_ref, reduced_other_ref, *refs
):
    outs, (windows, reduced, held, sems) = refs[:-4], refs[-4:]
    contract = (((0,), (0,)), ((), ()))
    tokens, hidden = mine_ref.shape
    hidden //= 2
    window = held.shape[0]
    blocks, block, _ = outs[0].shape
    offset = pl.multiple_of(at_ref[CORE] * hidden, 128)
    skips, copies = [], []
    for i, (n, j) in enumerate((n, j) for n in numbers for j in range(blocks)):
        first = at_ref[FIRST + blocks * n + j] * block
        start = pl.multiple_of(jnp.minimum(first // 128 * 128, hidden - window), 128)
        skips.append(pl.multiple_of(first - start, 16))
        copies.append(
            [
                pltpu.make_async_copy(
                    ref.at[:, pl.ds(pl.multiple_of(start + offset, 128), window)],
                    windows.at[i, pl.ds(side * tokens, tokens)],
                    sems.at[i, side],
                )
                for side, ref in enumerate((mine_ref, other_ref))
            ]
        )
        for copy in copies[-1]:
            copy.start()
    reduced[:tokens] = reduced_ref[...]
    reduced[tokens:] = reduced_other_ref[...]
    for i, skip in enumerate(skips):
        for copy in copies[i]:
            copy.wait()
        total = lax.dot_general(
            windows[i], reduced[...], contract, preferred_element_type=jnp.float32
        )
        held[...] = total.astype(held.dtype)
        outs[i // blocks][i % blocks] = held[pl.ds(skip, block)]


def diagonal_grad(numbers, table, mine, other, reduced, reduced_other):
    tokens, hidden = mine.shape
    columns = reduced.shape[1]
    out = jax.ShapeDtypeStruct((2, hidden // SIDE**2, columns), jnp.bfloat16)
    window = 896
    count = 2 * len(numbers)
    return pl.pallas_call(
        functools.partial(diagonal_kernel, numbers),
        in_specs=[SMEM] + [ANY] * 2 + [VMEM] * 2,
        out_specs=[VMEM] * len(numbers),
        out_shape=[out] * len(numbers),
        scratch_shapes=[
            pltpu.VMEM((count, 2 * tokens, window), jnp.bfloat16),
            pltpu.VMEM((2 * tokens, columns), jnp.bfloat16),
            pltpu.VMEM((window, columns), jnp.bfloat16),
            pltpu.SemaphoreType.DMA((count, 2)),
        ],
        cost_estimate=pl.CostEstimate(
            flops=4 * count * tokens * window * columns,
            bytes_accessed=4 * count * tokens * window,
            transcendentals=0,
        ),
        compiler_params=pltpu.CompilerParams(vmem_limit_bytes=50 << 20),
        name="diagonal_grad",
    )(table, mine, other, reduced, reduced_other)


def total_of(parts, *index):
    total = parts[0][index].astype(jnp.float32)
    for part in parts[1:]:
        total += part[index].astype(jnp.float32)
    return total


def half_kernel(at_ref, *refs):
    parts, out = refs[:4], refs[4]
    out[...] = total_of(parts, Ellipsis).astype(out.dtype)


def sum_half(table, parts, mine):
    blocks, block, columns = parts[0].shape
    half = pl.BlockSpec(
        (1, block, columns // 2),
        (lambda i, at: (i, 0, at[CORE])) if mine else (lambda i, at: (i, 0, 1 - at[CORE])),
    )
    out = pl.BlockSpec((1, block, columns // 2), lambda i, at: (i, 0, 0))
    return pl.pallas_call(
        half_kernel,
        grid_spec=pltpu.PrefetchScalarGridSpec(
            num_scalar_prefetch=1, grid=(blocks,), in_specs=[half] * len(parts), out_specs=out
        ),
        out_shape=jax.ShapeDtypeStruct((blocks, block, columns // 2), jnp.bfloat16),
        compiler_params=pltpu.CompilerParams(vmem_limit_bytes=20 << 20),
        name="sum_half",
    )(table, *parts)


def first_kernel(at_ref, *refs):
    sides, outs, held = refs[:2], refs[2:6], refs[6]
    rows = held.shape[1]
    for which in range(2):

        @pl.when(at_ref[CORE] == which)
        def _():
            for k in range(SIDE):
                block = sides[(k // 2 + which) % 2][k % 2]
                for i in range(SIDE):
                    held[SIDE * k + i] = block[i * rows : (i + 1) * rows]

    for t, out in enumerate(outs):
        for q in range(SIDE):
            out[q] = held[at_ref[FIRST_OUT + t] + q * at_ref[STRIDE]]


def first_parts(table, mine, other):
    _, block, half = mine.shape
    rows = block // SIDE
    return in_vmem(
        first_kernel, "first_parts",
        [jax.ShapeDtypeStruct((SIDE, rows, half), jnp.bfloat16)] * SIDE, mine, other,
        scratch=[pltpu.VMEM((SIDE**2, rows, half), jnp.bfloat16)], table=table,
    )


def second_kernel(at_ref, *refs):
    parts, outs = refs[:4], refs[4:]
    for t, out in enumerate(outs):
        out[...] = total_of(parts, at_ref[SECOND_OUT + t]).astype(out.dtype)


def second_parts(table, parts):
    shape = parts[0].shape[1:]
    return in_vmem(
        second_kernel, "second_parts",
        [jax.ShapeDtypeStruct(shape, jnp.float32)]
        + [jax.ShapeDtypeStruct(shape, jnp.bfloat16)] * (SIDE - 1),
        *parts, table=table,
    )


def cross(array, distance, diagonal_core):
    pairs = []
    for i in range(SIDE):
        for j in range(SIDE):
            for k in range(SIDE):
                for core in range(2):
                    to = [i, j, k]
                    for axis in (0, 1) if core == diagonal_core else (2,):
                        to[axis] = (to[axis] + distance) % SIDE
                    flat = [((p * SIDE + q) * SIDE + r) * 2 + core for p, q, r in ((i, j, k), to)]
                    pairs.append(tuple(flat))
    return lax.ppermute(array, ("y", "z", "x", "core"), pairs)


def stage_kernel(weight_ref, projector_ref, weight_out, projector_out, sems):
    copies = [
        pltpu.make_async_copy(weight_ref, weight_out, sems.at[0]),
        pltpu.make_async_copy(projector_ref, projector_out, sems.at[1]),
    ]
    for copy in copies:
        copy.start()
    for copy in copies:
        copy.wait()


def stage(weight, projector):
    return pl.pallas_call(
        stage_kernel,
        in_specs=[ANY] * 2,
        out_specs=[VMEM] * 2,
        out_shape=[
            jax.ShapeDtypeStruct(weight.shape, weight.dtype),
            jax.ShapeDtypeStruct(projector.shape, projector.dtype),
        ],
        scratch_shapes=[pltpu.SemaphoreType.DMA((2,))],
        compiler_params=pltpu.CompilerParams(vmem_limit_bytes=16 << 20),
        name="stage",
    )(weight, projector)


def update_kernel(
    at_ref, own_ref, own_far_ref, other_ref, other_far_ref, projector_ref, weight_ref, out_ref,
    quarters, direction,
):
    i = pl.program_id(0)
    rows, half = own_ref.shape
    depth = out_ref.shape[1]

    @pl.when(i == 0)
    def _():
        for which in range(2):

            @pl.when(at_ref[CORE] == which)
            def _():
                for near, far, place in (
                    (own_ref, own_far_ref, which), (other_ref, other_far_ref, 1 - which)
                ):
                    columns = pl.ds(place * half, half)
                    quarters[at_ref[QUARTER], :, columns] = near[...]
                    for t in range(1, SIDE):
                        quarters[at_ref[QUARTER + t], :, columns] = far[t - 1]

        for q in range(SIDE):
            direction[q * rows : (q + 1) * rows] = quarters[q]

    place = pl.ds(pl.multiple_of(at_ref[PLACE + i] * depth, depth), depth)
    delta = lax.dot_general(
        direction[...],
        projector_ref[pl.ds(pl.multiple_of(i * depth, depth), depth)],
        (((1,), (1,)), ((), ())),
        preferred_element_type=jnp.float32,
    )
    out_ref[...] = (weight_ref[:, place].astype(jnp.float32) - step_size * delta).astype(
        out_ref.dtype
    )


def update(table, own, own_far, other, other_far, projector, weight):
    block, width = weight.shape
    rank = projector.shape[1]
    rows = own.shape[0]
    parts = 8
    return pl.pallas_call(
        update_kernel,
        grid_spec=pltpu.PrefetchScalarGridSpec(
            num_scalar_prefetch=1,
            grid=(parts,),
            in_specs=[VMEM] * 6,
            out_specs=pl.BlockSpec((block, width // parts), lambda i, at: (0, at[PLACE + i])),
            scratch_shapes=[
                pltpu.VMEM((SIDE, rows, rank), own.dtype),
                pltpu.VMEM((block, rank), own.dtype),
            ],
        ),
        out_shape=jax.ShapeDtypeStruct(weight.shape, weight.dtype),
        compiler_params=pltpu.CompilerParams(vmem_limit_bytes=20 << 20),
        name="update",
    )(table, own, own_far, other, other_far, projector, weight)


def exchange(array, distance):
    pairs = []
    for i in range(SIDE):
        for j in range(SIDE):
            pairs.append(((SIDE * i + j) * 2, (SIDE * ((i - distance) % SIDE) + j) * 2))
            pairs.append(((SIDE * i + j) * 2 + 1, (SIDE * i + (j + distance) % SIDE) * 2 + 1))
    return lax.ppermute(array, ("y", "z", "core"), pairs)


def on_device(activations, out_grad, projector, weight, first_moment, second_moment):
    y, z, x, core = (lax.axis_index(name) for name in ("y", "z", "x", "core"))
    depth, rank = projector.shape
    half = rank // 2
    scale = 1.0 / math.sqrt(activations.shape[0] * SIDE**3 * 2)

    def own(array, axis):
        return lax.dynamic_slice_in_dim(array, core * half, half, axis)

    def others(array, axis):
        return lax.dynamic_slice_in_dim(array, (1 - core) * half, half, axis)

    def swap(array):
        return lax.ppermute(array, "core", SWAP)

    firsts = [
        SIDE * j + lax.rem(z - y + 2 * core + j + SIDE + distance, SIDE)
        for distance in DISTANCES
        for j in range(2)
    ]
    places = [
        2 * lax.rem(x + r, SIDE) + which for r in (0, 1, 3, 2) for which in (core, 1 - core)
    ]
    block_at = [lax.rem(y + t, SIDE) for t in range(SIDE)]
    quarter_at = [lax.rem(x + t, SIDE) for t in range(SIDE)]
    first_out = [jnp.where(core == 0, SIDE * p, q) for p, q in zip(block_at, quarter_at, strict=True)]
    second_out = [jnp.where(core == 0, q, p) for p, q in zip(block_at, quarter_at, strict=True)]
    table = jnp.stack([core, *firsts, *places, *first_out, 1 + 3 * core, *second_out, *quarter_at]).astype(jnp.int32)
    table, projector, out_grad = lax.optimization_barrier((table, projector, out_grad))

    def columns_of(place):
        return lax.dynamic_slice_in_dim(activations, places[place] * depth, depth, 1)

    def product(place, part):
        return jnp.dot(columns_of(place), part, preferred_element_type=jnp.float32)

    near = [hop(projector, "x", -1), hop(projector, "x", 1)]
    here = [projector, swap(projector)]
    other = swap(out_grad)
    total = product(0, here[0]) + product(1, here[1])
    near, total = lax.optimization_barrier((near, total))
    half_depth = depth // 2
    far = [hop(near[1][:half_depth], "x", 1), hop(near[0][half_depth:], "x", -1)]
    near = [near[0], swap(near[0]), near[1], swap(near[1])]
    for place, part in enumerate(near):
        total += product(2 + place, part)
    last = [columns_of(6), columns_of(7)]
    far, total, last = lax.optimization_barrier((far, total, last))
    far = [jnp.concatenate(far, axis=0)]
    far += [swap(far[0])]
    for columns, part in zip(last, far, strict=True):
        total += jnp.dot(columns, part, preferred_element_type=jnp.float32)
    reduced = total.astype(jnp.bfloat16)
    reduced_other = swap(reduced)

    first_moment, second_moment, _ = lax.optimization_barrier(
        (first_moment, second_moment, near[0])
    )
    moments = jnp.stack([first_moment, second_moment])
    rows = moments.shape[1]
    moments_other = swap(others(moments, 2))
    moments_own = own(moments, 2)
    moments = jnp.where(
        core == 0,
        jnp.concatenate([moments_own, moments_other], axis=1),
        jnp.concatenate([moments_other, moments_own], axis=1),
    )
    weight, _ = lax.optimization_barrier((weight, far[0]))
    weight_all = lax.all_gather(weight, ("x", "core"), axis=0, tiled=True)

    sums = []
    for number, distance in enumerate(DISTANCES):
        (part,) = diagonal_grad((number,), table, out_grad, other, reduced, reduced_other)
        sums.append(exchange(part, distance) if distance else part)
    parts = [*here, *near, *far]
    sums[3], parts = lax.optimization_barrier((sums[3], parts))
    projector_all = jnp.concatenate(parts, axis=0)
    sums[0], projector_all, weight_all, moments = lax.optimization_barrier(
        (sums[0], projector_all, weight_all, moments)
    )
    other = sum_half(table, sums, False)
    sums[0], other = lax.optimization_barrier((sums[0], other))
    mine = sum_half(table, sums, True)
    sums = first_parts(table, mine, swap(other))
    sums = [sums[0], *(cross(sums[t], t, 0) for t in (2, 1, 3))]
    sums = second_parts(table, sums)
    sums = [sums[0], *(cross(sums[t], t, 1) for t in (2, 1, 3))]
    grad = sum(part.astype(jnp.float32) for part in sums)
    grad = grad * scale

    new_first = beta_first * moments[0] + (1.0 - beta_first) * grad
    new_second = beta_second * moments[1] + (1.0 - beta_second) * grad * grad
    direction = (
        new_first / correct_first / (jnp.sqrt(new_second / correct_second) + epsilon)
    ).astype(jnp.bfloat16)

    direction, projector_all, weight_all = lax.optimization_barrier(
        (direction, projector_all, weight_all)
    )
    weight_all, projector_all = stage(weight_all.T, projector_all)
    far = [hop(direction, "x", -t) for t in (2, 1, 3)]
    other = swap(direction)
    far, weight_all, projector_all = lax.optimization_barrier((far, weight_all, projector_all))
    far = jnp.stack([far[1], far[0], far[2]])
    other_far = swap(far)
    new_weight = update(table, direction, far, other, other_far, projector_all, weight_all).T
    new_first, new_second, _ = lax.optimization_barrier((new_first, new_second, far))

    news = jnp.stack([new_first, new_second])
    kept = lax.dynamic_slice_in_dim(news, core * rows, rows, 1)
    came = swap(lax.dynamic_slice_in_dim(news, (1 - core) * rows, rows, 1))
    news = jnp.where(
        core == 0,
        jnp.concatenate([kept, came], axis=2),
        jnp.concatenate([came, kept], axis=2),
    )
    return (new_weight, news[0], news[1])


def solution(mesh):
    grid = Mesh(mesh.devices.reshape(SIDE, SIDE, SIDE, 2), ("y", "z", "x", "core"))
    everywhere, group = ("y", "z", "x", "core"), ("x", "core")
    in_specs = (
        P(everywhere, None),
        P(everywhere, None),
        P(group, None),
        P(group, ("y", "z")),
        P(everywhere, None),
        P(everywhere, None),
    )
    out_specs = (P(None, ("y", "z")), P(everywhere, None), P(everywhere, None))
    return jax.shard_map(
        on_device, mesh=grid, in_specs=in_specs, out_specs=out_specs, check_vma=False
    )
```
